128 devices in a mesh: dp: 32 (over x, y, core), mp: 4 (over z).
Axes of the slice: x: 4, y: 4, z: 4, core: 2. Of those that a mesh axis runs over, the one named last changes fastest.
Arguments:
- qkv: bfloat16 [24576, 3, 3072], P('dp', None, 'mp'), may hold values from -128 to 128, as said below
- segment_ids: int32 [24576], P('dp'), may hold values from -1 to 191, as said below
- block_dest: int32 [192], replicated, may hold values from 0 to 191, as said below
- q_gain: float32 [3072], P('mp'), may hold values from 0.5 to 5.2, as said below
- k_gain: float32 [3072], P('mp'), may hold values from 0.5 to 5.2, as said below
- out_weight: bfloat16 [3072, 3072], P(None, 'mp'), may hold values from -0.5 to 0.5
- cotangent: bfloat16 [24576, 3072], P(('dp', 'mp')), may hold values from -24 to 24
Outputs:
- attn_out: bfloat16 [24576, 3072], P(('dp', 'mp'))
- qkv_grad: bfloat16 [24576, 3, 3072], P('dp', None, 'mp')
- w_grad: float32 [3072, 3072], P('dp', 'mp')
The draws below stay inside these ranges and needn't reach their ends.
Inputs may be any that keep to these rules, and one draw needn't show every extreme that they name: `block_dest`: A permutation of the 192 block positions; position p lies on dp index p // 6. No dp index sends two blocks to the same dp index, and every image's blocks take consecutive positions of one dp index. `segment_ids`: each block belongs to one image; an image's blocks are full except its last, which holds 4 to 127 real rows followed by padding rows (-1). `qkv`: entries of the query and key parts have row and column scales of their own; values of order one. `q_gain`: Positive. `k_gain`: Positive.
All inputs are finite; a program needn't handle non-finite values.
Results may differ from the reference program's by a relative error of at most 0.02.
The reference program's roundings to bfloat16 on the way count: a program that leaves them out, or rounds other values in their place, can miss the bound.
Values may be sent and summed in bfloat16 or wider, within the bound.
No kernel may reach another device: no remote copies, remote signals or barrier semaphores. Data moves between devices by JAX's collectives and lax.ppermute only.
A program may use at most 192 MiB of HBM per device.

```python
import math
import jax
import jax.numpy as jnp
from jax import lax

HEADS = 24
HD = 128
D_OUT = 3072
BLK = 128
BLK_DEV = 6
TOKENS = 24576
N_DP = 32
N_MP = 4


def block_plan(key):
    subkeys = jax.random.split(key, 7)
    positions = jnp.arange(BLK_DEV, dtype=jnp.int32)
    devices = jnp.arange(N_DP, dtype=jnp.int32)
    cut_draw = jax.random.randint(subkeys[0], (N_DP, BLK_DEV), 0, 5)
    starred = jax.random.randint(subkeys[1], (), 0, N_DP - 1)
    starts = (cut_draw < 2) & (devices[:, None] != starred)
    starts = starts | (positions[None, :] == 0)
    starts = starts | (devices[:, None] == N_DP - 1) & (positions[None, :] == BLK_DEV - 1)
    first_pos = lax.cummax(jnp.where(starts, positions[None, :], 0), axis=1)
    image_ids = devices[:, None] * BLK_DEV + first_pos
    next_start = jnp.concatenate([starts[:, 1:], jnp.ones((N_DP, 1), jnp.bool_)], axis=1)
    tail_rows = jax.random.randint(subkeys[2], (N_DP, BLK_DEV), 4, BLK)
    valid_rows = jnp.where(next_start, tail_rows, BLK)
    row_ids = jnp.arange(BLK, dtype=jnp.int32)
    seg_bal = jnp.where(row_ids[None, None, :] < valid_rows[:, :, None], image_ids[:, :, None], -1)
    relabel = jax.random.permutation(subkeys[3], N_DP)
    order_perm = jax.random.permutation(subkeys[4], N_DP)
    offsets = jax.random.permutation(subkeys[5], N_DP)[:BLK_DEV]
    sources = relabel[(order_perm[:, None] + offsets[None, :]) % N_DP]

    def slot_order(slot_key):
        return jax.random.permutation(slot_key, BLK_DEV)
    slot_perm = jax.vmap(slot_order)(jax.random.split(subkeys[6], N_DP))
    slot_ids = slot_perm[sources, positions[None, :]]
    anchor = (sources * BLK_DEV + slot_ids).reshape(-1)
    dest_ids = (devices[:, None] * BLK_DEV + positions[None, :]).reshape(-1)
    block_dest = jnp.zeros((N_DP * BLK_DEV,), jnp.int32).at[anchor].set(dest_ids)
    seg_orig = jnp.zeros((N_DP * BLK_DEV, BLK), jnp.int32).at[anchor].set(seg_bal.reshape(-1, BLK))
    return (block_dest, seg_orig.reshape(-1))


def draw_block_dest(key, part):
    return block_plan(key)[0]


def draw_segment_ids(key, part):
    return block_plan(key)[1]


def gain_draw(key):
    jitter = jax.random.uniform(key, (HEADS, HD), jnp.float32, -0.5, 0.5)
    return jnp.exp(jitter).reshape(-1)


def draw_q_gain(key, part):
    key = jax.random.fold_in(key, 21)
    return gain_draw(key)


def draw_k_gain(key, part):
    key = jax.random.fold_in(key, 22)
    return gain_draw(key)


def draw_qkv(key, part):
    key = jax.random.fold_in(key, 11)
    subkeys = jax.random.split(key, 3)
    col_width = HEADS * HD
    normal_part = jnp.clip(jax.random.normal(subkeys[0], (TOKENS, 3, col_width), jnp.float32), -4.0, 4.0)
    kind_ids = jnp.arange(3)[None, :, None]
    row_scale = jnp.exp(jax.random.uniform(subkeys[1], (TOKENS, 3, 1), jnp.float32, math.log(0.3), math.log(3.0)))
    col_scale = jnp.exp(jax.random.uniform(subkeys[2], (1, 3, col_width), jnp.float32, math.log(0.3), math.log(3.0)))
    values = jnp.where(kind_ids == 2, normal_part, normal_part * row_scale * col_scale)
    return values.astype(jnp.bfloat16)


def raised(values, rng, source, target, shards_of, factor):
    def block_of(axis_at):
        return (jnp.arange(values.shape[axis_at]) // (values.shape[axis_at] // shards_of)).reshape((-1,) + (1,) * (values.ndim - 1 - axis_at))

    near = jax.random.permutation(rng, shards_of)[block_of(target)]
    second = (block_of(target) + shards_of // 2) % shards_of
    return jnp.where((block_of(source) == near) | (block_of(source) == second), factor * values, values)


def block_levels(own_key, shape, cuts, least, high):
    gain, own = 1.0, jax.random.fold_in(own_key, 6)
    for dim, parts in cuts:
        draws = jnp.exp(jax.random.uniform(jax.random.fold_in(own, dim), (parts,), jnp.float32, least / len(cuts), high / len(cuts)))
        gain = gain * jnp.repeat(draws, shape[dim] // parts).reshape([-1 if axis == dim else 1 for axis in range(len(shape))])
    return gain


def normal_values(stream_key, extent, deviation, most, cuts=(), kind=jnp.bfloat16):
    entries = deviation * jax.random.normal(stream_key, extent, jnp.float32)
    if cuts:
        entries = entries * block_levels(stream_key, extent, cuts, -0.22, 0.18)
    return jnp.clip(entries, -most, most).astype(kind)


def gaussian_with(rng, shape, width, most, cuts, heavy, kind=jnp.bfloat16):
    values = width * jax.random.normal(rng, shape, jnp.float32)
    if cuts:
        values = values * block_levels(rng, shape, cuts, -0.22, 0.18)
    return jnp.clip(raised(values, jax.random.fold_in(rng, 3), *heavy), -most, most).astype(kind)


def setup_inputs(seed: int = 0) -> dict:
    splits = jax.random.split(jax.random.key(seed), 8)
    qkv = draw_qkv(jax.random.fold_in(splits[7], 71), 0)
    segment_ids = draw_segment_ids(jax.random.fold_in(splits[7], 71), 0)
    block_dest = draw_block_dest(jax.random.fold_in(splits[7], 71), 0)
    q_gain = draw_q_gain(jax.random.fold_in(splits[7], 71), 0)
    k_gain = draw_k_gain(jax.random.fold_in(splits[7], 71), 0)
    out_weight = normal_values(splits[5], (D_OUT, HEADS * HD), HD ** -0.5, 0.5, ((1, 4),))
    cotangent = gaussian_with(splits[6], (TOKENS, D_OUT), 1.0, 24.0, ((0, 128),), (0, 1, 128, 5.5))
    return {"qkv": qkv, "segment_ids": segment_ids, "block_dest": block_dest, "q_gain": q_gain, "k_gain": k_gain, "out_weight": out_weight, "cotangent": cotangent}


NORM_EPS = 1e-06
MASKED_SCORE = -1e+30

def dot_first(left, right):
    return lax.dot_general(left, right, (((0,), (0,)), ((), ())), preferred_element_type=jnp.float32)

def dot_last(left, right):
    return lax.dot_general(left, right, (((1,), (1,)), ((), ())), preferred_element_type=jnp.float32)

def layer_norm(inputs, norm_gain):
    values = inputs.astype(jnp.float32)
    centred = values - lax.optimization_barrier(jnp.mean(values, axis=1, keepdims=True))
    inv_scale = lax.rsqrt(lax.optimization_barrier(jnp.mean(centred * centred, axis=1, keepdims=True)) + NORM_EPS)
    normed = centred * inv_scale
    return (normed, inv_scale, (normed * norm_gain[None, :]).astype(jnp.bfloat16))

def norm_backward(upstream, normed, inv_scale, norm_gain):
    scaled = upstream * norm_gain[None, :]
    centred = scaled - lax.optimization_barrier(jnp.mean(scaled, axis=1, keepdims=True))
    projection_term = normed * lax.optimization_barrier(jnp.mean(scaled * normed, axis=1, keepdims=True))
    return (inv_scale * (centred - projection_term)).astype(jnp.bfloat16)

def head_pass(queries, key_rows, value_rows, q_scale, k_scale, segments, head_grad):
    factor = 1.0 / math.sqrt(queries.shape[1])
    q_normed, q_inv, q_hat = layer_norm(queries, q_scale)
    k_normed, k_inv, k_hat = layer_norm(key_rows, k_scale)
    scores = dot_last(q_hat, k_hat) * factor
    allowed = (segments[:, None] == segments[None, :]) & (segments[None, :] >= 0)
    masked = jnp.where(allowed, scores, MASKED_SCORE)
    row_top = lax.optimization_barrier(jnp.max(masked, axis=1, keepdims=True))
    weights = jnp.exp(masked - row_top) * allowed.astype(jnp.float32)
    totals = jnp.maximum(lax.optimization_barrier(jnp.sum(weights, axis=1, keepdims=True)), 1.0)
    weights_bf = (weights / totals).astype(jnp.bfloat16)
    attended = jnp.dot(weights_bf, value_rows, preferred_element_type=jnp.float32).astype(jnp.bfloat16)
    value_grad = dot_first(weights_bf, head_grad).astype(jnp.bfloat16)
    prob_grad = dot_last(head_grad, value_rows)
    row_delta = lax.optimization_barrier(jnp.sum(head_grad.astype(jnp.float32) * attended.astype(jnp.float32), axis=1, keepdims=True))
    score_grad = (weights_bf.astype(jnp.float32) * (prob_grad - row_delta)).astype(jnp.bfloat16)
    qn_grad = jnp.dot(score_grad, k_hat, preferred_element_type=jnp.float32) * factor
    kn_grad = dot_first(score_grad, q_hat) * factor
    query_grad = norm_backward(qn_grad, q_normed, q_inv, q_scale)
    key_grad = norm_backward(kn_grad, k_normed, k_inv, k_scale)
    return (attended, query_grad, key_grad, value_grad)

def reference(qkv, segment_ids, block_dest, q_gain, k_gain, out_weight, cotangent):
    block_count = block_dest.shape[0]
    anchor = jnp.zeros((block_count,), jnp.int32).at[block_dest].set(jnp.arange(block_count, dtype=jnp.int32))
    per_device = BLK_DEV * BLK
    col_width = HEADS * HD
    group_width = col_width // N_MP
    balanced = qkv.reshape(block_count, BLK, 3, col_width)[anchor].reshape(N_DP, per_device, 3, col_width)
    segments = segment_ids.reshape(block_count, BLK)[anchor].reshape(N_DP, per_device)
    grad_blocks = cotangent.reshape(N_DP, per_device, D_OUT)

    def group_pass(weight_sum, pieces):
        rows_qkv, row_segments, grad_rows = pieces
        out_grad = jnp.dot(grad_rows, out_weight, preferred_element_type=jnp.float32).astype(jnp.bfloat16)
        attended_parts, query_parts, key_parts, value_parts = ([], [], [], [])
        for head_idx in range(HEADS):
            first_col = head_idx * HD
            columns = slice(first_col, first_col + HD)
            result = head_pass(rows_qkv[:, 0, columns], rows_qkv[:, 1, columns], rows_qkv[:, 2, columns], q_gain[columns], k_gain[columns], row_segments, out_grad[:, columns])
            attended_parts.append(result[0])
            query_parts.append(result[1])
            key_parts.append(result[2])
            value_parts.append(result[3])
        attended = jnp.concatenate(attended_parts, axis=1)
        projected = jnp.zeros((per_device, D_OUT), jnp.float32)
        for group_idx in range(N_MP):
            group_cols = slice(group_idx * group_width, (group_idx + 1) * group_width)
            rounded = dot_last(attended[:, group_cols], out_weight[:, group_cols]).astype(jnp.bfloat16)
            rounded = lax.optimization_barrier(rounded)
            projected = projected + rounded.astype(jnp.float32)
        weight_sum = weight_sum + dot_first(grad_rows, attended)
        grads = jnp.stack([jnp.concatenate(query_parts, axis=1), jnp.concatenate(key_parts, axis=1), jnp.concatenate(value_parts, axis=1)], axis=1)
        return (weight_sum, (projected.astype(jnp.bfloat16), grads))
    start_sum = jnp.zeros((D_OUT, col_width), jnp.float32)
    w_grad, outputs = lax.scan(group_pass, start_sum, (balanced, segments, grad_blocks))
    attn_out = outputs[0].reshape(N_DP * per_device, D_OUT)
    qkv_grad = outputs[1].reshape(N_DP * per_device, 3, col_width)
    return (attn_out, qkv_grad, w_grad)
```

```python
import functools
import math

import jax
import jax.numpy as jnp
from jax import lax
from jax.experimental import pallas as pl
from jax.experimental.pallas import tpu as pltpu
from jax.sharding import Mesh
from jax.sharding import PartitionSpec as P

HD = 128
BLK = 128


NORM_EPS = 1e-06
MASKED_SCORE = -1e30
LOG2_E = math.log2(math.e)
DP = ("x", "y", "core")
FORWARD_ROWS = 384
FORWARD_HEADS = 3
BACKWARD_ROWS = 768
VMEM_LIMIT = 56 * 1024 * 1024
LITTLE = pl.CostEstimate(flops=1, bytes_accessed=1, transcendentals=0)
LARGE = pl.CostEstimate(flops=10**12, bytes_accessed=10**9, transcendentals=0)


def dot_first(left, right):
    return lax.dot_general(
        left, right, (((0,), (0,)), ((), ())), preferred_element_type=jnp.float32
    )


def dot_last(left, right):
    return lax.dot_general(
        left, right, (((1,), (1,)), ((), ())), preferred_element_type=jnp.float32
    )


def layer_norm(values, norm_gain):
    centred = values - jnp.mean(values, axis=1, keepdims=True)
    inv_scale = lax.rsqrt(jnp.mean(centred * centred, axis=1, keepdims=True) + NORM_EPS)
    normed = centred * inv_scale
    return (normed, inv_scale, (normed * norm_gain).astype(jnp.bfloat16))


def norm_backward(upstream, normed, inv_scale, norm_gain):
    scaled = upstream * norm_gain
    centred = scaled - jnp.mean(scaled, axis=1, keepdims=True)
    projection_term = normed * jnp.mean(scaled * normed, axis=1, keepdims=True)
    return (inv_scale * (centred - projection_term)).astype(jnp.bfloat16)


def in_row_order(ref, columns):
    cuts, span, _ = ref.shape[0], ref.shape[3], ref.shape[4]
    rows8 = BLK // cuts
    tiles = ref[:, 0, 0, :, columns].astype(jnp.float32).reshape(cuts, span // rows8, rows8, HD)
    return jnp.concatenate(
        [tiles[:, pos].reshape(BLK, HD) for pos in range(span // rows8)], axis=0
    )


def forward_kernel(
    groups, here_ref, q_ref, k_ref, v_ref, seg_col, seg_row, qg_ref, kg_ref, weight_ref,
    att_ref, prob_ref, *refs,
):
    at_step = pl.program_id(0)
    rows, width = att_ref.shape[0], q_ref.shape[-1]

    def attend(group):
        factor = LOG2_E / math.sqrt(HD)
        keys_image = seg_row[...]
        keys_image = jnp.where(keys_image >= 0, keys_image, -2)
        heads = [slice(first, first + HD) for first in range(0, width, HD)]
        q_hats = [layer_norm(in_row_order(q_ref, at), qg_ref[:, at])[2] for at in heads]
        k_hats = [layer_norm(in_row_order(k_ref, at), kg_ref[:, at])[2] for at in heads]
        values = [in_row_order(v_ref, at).astype(jnp.bfloat16) for at in heads]
        tasks = [
            (head, slice(start, start + FORWARD_ROWS))
            for head in range(len(heads))
            for start in range(0, rows, FORWARD_ROWS)
        ]

        def scores_of(head, block):
            return dot_last(q_hats[head][block], k_hats[head])

        ready = scores_of(*tasks[0])
        for at, (head, block) in enumerate(tasks):
            scores = ready
            if at + 1 < len(tasks):
                ready = scores_of(*tasks[at + 1])
            image = seg_col[block]
            masked = jnp.where(image == keys_image, scores, MASKED_SCORE)
            top = jnp.max(masked, axis=1, keepdims=True)
            weights = jnp.exp2((masked - top) * factor)
            totals = jnp.maximum(jnp.sum(weights, axis=1, keepdims=True), 1.0)
            scale = jnp.where(image >= 0, 1.0 / totals, 0.0)
            probs = (weights * scale).astype(jnp.bfloat16)
            prob_ref[head, block] = probs
            first = group * width + head * HD
            att_ref[block, first : first + HD] = jnp.dot(
                probs, values[head], preferred_element_type=jnp.float32
            ).astype(jnp.bfloat16)

    for group in range(groups):
        pl.when(at_step == group)(functools.partial(attend, group))

    part_refs, back_ref, turned = refs[:-2], refs[-2], refs[-1]
    places = len(part_refs)
    share = rows // places

    @pl.when(at_step == groups)
    def _():
        for by in range(places):
            first = pl.multiple_of((here_ref[0] + by) % places * share, share)
            block = att_ref[pl.ds(first, share)]
            turned[by * share : (by + 1) * share] = block
            back = (places - by) % places
            back_ref[back * share : (back + 1) * share] = block

    @pl.when(at_step >= groups)
    def _():
        sums = dot_last(turned[...], weight_ref[...]).astype(jnp.bfloat16)
        for by, part_ref in enumerate(part_refs):
            part_ref[...] = sums[by * share : (by + 1) * share]


def backward_kernel(step, q_ref, k_ref, v_ref, prob_ref, grad_ref, att_ref, qg_ref, kg_ref, out_ref):
    factor = 1.0 / math.sqrt(HD)
    q_normed, q_inv, q_hat = layer_norm(in_row_order(q_ref, slice(0, HD)), qg_ref[...])
    k_normed, k_inv, k_hat = layer_norm(in_row_order(k_ref, slice(0, HD)), kg_ref[...])
    values = in_row_order(v_ref, slice(0, HD)).astype(jnp.bfloat16)
    rows = att_ref.shape[0]
    key_sum = jnp.zeros((HD, rows), jnp.float32)
    value_sum = jnp.zeros((HD, rows), jnp.float32)
    for start in range(0, rows, step):
        block = slice(start, start + step)
        grads = grad_ref[block]
        wide = grads.astype(jnp.float32)
        probs = prob_ref[0, block]
        delta = jnp.sum(wide * att_ref[block].astype(jnp.float32), axis=1, keepdims=True)
        prob_grad = dot_last(grads, values)
        score_grad = (probs.astype(jnp.float32) * (prob_grad - delta)).astype(jnp.bfloat16)
        qn_grad = jnp.dot(score_grad, k_hat, preferred_element_type=jnp.float32) * factor
        out_ref[0, block] = norm_backward(qn_grad, q_normed[block], q_inv[block], qg_ref[...])
        value_sum += jnp.dot(
            wide.T.astype(jnp.bfloat16), probs, preferred_element_type=jnp.float32
        )
        key_sum += jnp.dot(
            q_hat[block].astype(jnp.float32).T.astype(jnp.bfloat16),
            score_grad,
            preferred_element_type=jnp.float32,
        )
    out_ref[2] = value_sum.T.astype(jnp.bfloat16)
    out_ref[1] = norm_backward(key_sum.T * factor, k_normed, k_inv, kg_ref[...])


def part_specs(cuts, span, groups, width):
    per_half = groups // 2

    def spec(part):
        def place(step, *_):
            group = jnp.minimum(step, groups - 1)
            return (0, group // per_half, part, 0, group % per_half)

        return pl.BlockSpec((cuts, 1, 1, span, width), place)

    return [spec(part) for part in range(3)]


def attention_forward(landed, segments, q_gain, k_gain, out_weight, here, places):
    cuts, _, _, span, half = landed.shape
    rows, heads = cuts * span, 2 * half // HD
    groups, width = heads // FORWARD_HEADS, FORWARD_HEADS * HD
    d_out = out_weight.shape[0]
    blocks = 4
    share = rows // places
    gain_spec = pl.BlockSpec((1, width), lambda step, here: (0, jnp.minimum(step, groups - 1)))

    def column(step):
        return jnp.maximum(step - groups, 0)

    return pl.pallas_call(
        functools.partial(forward_kernel, groups),
        grid_spec=pltpu.PrefetchScalarGridSpec(
        num_scalar_prefetch=1,
        grid=(groups + blocks,),
        in_specs=part_specs(cuts, span, groups, width)
        + [
            pl.BlockSpec((rows, 1), lambda step, here: (0, 0)),
            pl.BlockSpec((1, rows), lambda step, here: (0, 0)),
            gain_spec,
            gain_spec,
            pl.BlockSpec((d_out // blocks, heads * HD), lambda step, here: (column(step), 0)),
        ],
        out_specs=[
            pl.BlockSpec((rows, heads * HD), lambda step, here: (0, 0)),
            pl.BlockSpec(
                (FORWARD_HEADS, rows, rows), lambda step, here: (jnp.minimum(step, groups - 1), 0, 0)
            ),
        ]
        + [pl.BlockSpec((share, d_out // blocks), lambda step, here: (0, column(step)))] * places
        + [pl.BlockSpec((rows, heads * HD), lambda step, here: (0, 0))],
        scratch_shapes=[pltpu.VMEM((rows, heads * HD), jnp.bfloat16)],
        ),
        out_shape=[
            jax.ShapeDtypeStruct((rows, heads * HD), jnp.bfloat16),
            jax.ShapeDtypeStruct((heads, rows, rows), jnp.bfloat16),
        ]
        + [jax.ShapeDtypeStruct((share, d_out), jnp.bfloat16)] * places
        + [jax.ShapeDtypeStruct((rows, heads * HD), jnp.bfloat16)],
        compiler_params=pltpu.CompilerParams(vmem_limit_bytes=VMEM_LIMIT),
        cost_estimate=pl.CostEstimate(
            flops=4 * heads * rows * rows * HD + 2 * rows * d_out * heads * HD,
            bytes_accessed=2 * heads * rows * (rows + 4 * HD) + 4 * rows * d_out,
            transcendentals=heads * rows * rows,
        ),
        name="attention_forward",
    )(
        here.reshape(1).astype(jnp.int32),
        landed,
        landed,
        landed,
        segments[:, None],
        segments[None, :],
        q_gain[None, :],
        k_gain[None, :],
        out_weight,
    )


def attention_backward(landed, probs, out_grad, attended, q_gain, k_gain):
    cuts, _, _, span, half = landed.shape
    rows, heads = cuts * span, 2 * half // HD
    gain_spec = pl.BlockSpec((1, HD), lambda head: (0, head))
    row_spec = pl.BlockSpec((rows, HD), lambda head: (0, head))
    return pl.pallas_call(
        functools.partial(backward_kernel, BACKWARD_ROWS),
        grid=(heads,),
        in_specs=part_specs(cuts, span, heads, HD)
        + [
            pl.BlockSpec((1, rows, rows), lambda head: (head, 0, 0)),
            row_spec,
            row_spec,
            gain_spec,
            gain_spec,
        ],
        out_specs=pl.BlockSpec((3, rows, HD), lambda head: (0, 0, head)),
        out_shape=jax.ShapeDtypeStruct((3, rows, heads * HD), jnp.bfloat16),
        compiler_params=pltpu.CompilerParams(vmem_limit_bytes=VMEM_LIMIT),
        cost_estimate=LARGE,
        name="attention_backward",
    )(landed, landed, landed, probs, out_grad, attended, q_gain[None, :], k_gain[None, :])


def cut_kernel(rows_ref, out_ref):
    cuts, span = out_ref.shape[0], out_ref.shape[3]
    rows8 = BLK // cuts
    tiles = rows_ref[0].astype(jnp.float32).reshape(span // rows8, cuts, rows8, -1)
    for cut in range(cuts):
        out_ref[cut, 0, 0] = tiles[:, cut].reshape(span, -1).astype(jnp.bfloat16)


def cut_blocks(planes, cuts):
    parts, rows, width = planes.shape
    span, half = rows // cuts, width // 2
    return pl.pallas_call(
        cut_kernel,
        grid=(parts, 2),
        in_specs=[pl.BlockSpec((1, rows, half), lambda part, side: (part, 0, side))],
        out_specs=pl.BlockSpec(
            (cuts, 1, 1, span, half), lambda part, side: (0, side, part, 0, 0)
        ),
        out_shape=jax.ShapeDtypeStruct((cuts, 2, parts, span, half), jnp.bfloat16),
        compiler_params=pltpu.CompilerParams(vmem_limit_bytes=VMEM_LIMIT),
        cost_estimate=pl.CostEstimate(
            flops=0, bytes_accessed=4 * parts * rows * width, transcendentals=0
        ),
        name="cut_blocks",
    )(planes)


def grad_kernel(here_ref, *refs):
    pieces, (weight_ref, grad_ref, columns_ref, total) = refs[:-4], refs[-4:]
    places, step = len(pieces), pl.program_id(0)
    rows = jnp.concatenate([piece[...].astype(jnp.float32) for piece in pieces], axis=0)
    columns_ref[...] = rows.T.astype(jnp.bfloat16)
    product = jnp.dot(
        rows.astype(jnp.bfloat16), weight_ref[...], preferred_element_type=jnp.float32
    )

    @pl.when(step == 0)
    def _():
        total[...] = product

    @pl.when(step > 0)
    def _():
        total[...] += product

    @pl.when(step == pl.num_programs(0) - 1)
    def _():
        share = pieces[0].shape[0]
        for back in range(places):
            first = pl.multiple_of((here_ref[0] + places - back) % places * share, share)
            grad_ref[pl.ds(first, share)] = total[back * share : (back + 1) * share].astype(
                jnp.bfloat16
            )


def grad_products(here, pieces, out_weight):
    places = len(pieces)
    share, d_out = pieces[0].shape
    width = out_weight.shape[1]
    rows, step = places * share, 768
    return pl.pallas_call(
        grad_kernel,
        grid_spec=pltpu.PrefetchScalarGridSpec(
            num_scalar_prefetch=1,
            grid=(d_out // step,),
            in_specs=[pl.BlockSpec((share, step), lambda at, here: (0, at))] * places
            + [pl.BlockSpec((step, width), lambda at, here: (at, 0))],
            out_specs=[
                pl.BlockSpec((rows, width), lambda at, here: (0, 0)),
                pl.BlockSpec((step, rows), lambda at, here: (at, 0)),
            ],
            scratch_shapes=[pltpu.VMEM((rows, width), jnp.float32)],
        ),
        out_shape=[
            jax.ShapeDtypeStruct((rows, width), jnp.bfloat16),
            jax.ShapeDtypeStruct((d_out, rows), jnp.bfloat16),
        ],
        compiler_params=pltpu.CompilerParams(vmem_limit_bytes=VMEM_LIMIT),
        cost_estimate=LITTLE,
        name="grad_products",
    )(here.reshape(1).astype(jnp.int32), *pieces, out_weight)


def weight_kernel(core_ref, cot_ref, att_ref, out_ref):
    peers, _, share, rows = cot_ref.shape
    terms = jnp.dot(
        cot_ref[...].reshape(peers * share, rows),
        att_ref[...],
        preferred_element_type=jnp.float32,
    )
    out_ref[...] = terms.astype(jnp.bfloat16).reshape(out_ref.shape)


def weight_terms(parity, grad_columns, attended, peers):
    d_out, rows = grad_columns.shape
    width = attended.shape[1]
    share = d_out // peers
    step = peers // 4
    block = pl.BlockSpec((step, share, width), lambda at, core: (at, 0, 0))
    return pl.pallas_call(
        weight_kernel,
        grid_spec=pltpu.PrefetchScalarGridSpec(
            num_scalar_prefetch=1,
            grid=(2,),
            in_specs=[
                pl.BlockSpec((step, 1, share, rows), lambda at, core: (at, core[0], 0, 0)),
                pl.BlockSpec((rows, width), lambda at, core: (0, 0)),
            ],
            out_specs=block,
        ),
        out_shape=jax.ShapeDtypeStruct((peers // 2, share, width), jnp.bfloat16),
        compiler_params=pltpu.CompilerParams(vmem_limit_bytes=VMEM_LIMIT),
        cost_estimate=LARGE,
        name="weight_terms",
    )(
        parity.reshape(1).astype(jnp.int32),
        grad_columns.reshape(peers // 2, 2, share, rows),
        attended,
    )


def turn(size, by):
    return [(at, (at + by) % size) for at in range(size)]


def gathered(own, axis):
    size = lax.axis_size(axis)
    return jnp.stack([own] + [lax.ppermute(own, axis, turn(size, by)) for by in range(1, size)])


def body(qkv, segment_ids, block_dest, q_gain, k_gain, out_weight, cotangent):
    peers = lax.axis_size(DP)
    my_index = lax.axis_index(DP)
    row_count, parts_qkv, col_width = qkv.shape
    per_device = row_count // BLK
    n_blocks = block_dest.shape[0]
    cuts = peers // 2
    rows8 = BLK // cuts
    half = col_width // 2

    all_ids = jnp.arange(n_blocks, dtype=jnp.int32)
    source_of = jnp.sum(
        (block_dest[None, :] == all_ids[:, None]).astype(jnp.int32) * all_ids[None, :], axis=1
    )
    size_x, size_y, size_core = (lax.axis_size(axis) for axis in DP)
    here_x, here_y, here_core = (lax.axis_index(axis) for axis in DP)
    seg_plane = gathered(gathered(segment_ids.reshape(per_device, BLK), "core"), "y")
    seg_plane = seg_plane.reshape(size_y * size_core * per_device, BLK)

    sources = source_of.reshape(peers, 1, per_device)
    part_ids = jnp.arange(parts_qkv, dtype=jnp.int32)[None, :, None]
    piece_of = (
        (sources // per_device) * (parts_qkv * per_device)
        + part_ids * per_device
        + sources % per_device
    ).reshape(-1)

    places = lax.axis_size("mp")
    here = lax.axis_index("mp")
    pieces_cot = [cotangent] + [
        lax.ppermute(cotangent, "mp", turn(places, by)) for by in range(1, places)
    ]

    planes = jnp.transpose(qkv, (1, 0, 2))
    pieces = cut_blocks(planes, cuts).reshape(peers, parts_qkv, per_device * rows8, half)
    spread = lax.all_to_all(pieces, DP, split_axis=0, concat_axis=0, tiled=True)
    ordered = jnp.take(
        spread.reshape(n_blocks * parts_qkv, rows8, half), piece_of, axis=0, mode="clip"
    ).reshape(pieces.shape)
    near = (pieces_cot[1], pieces_cot[places - 1])
    ordered, seg_plane, near = lax.optimization_barrier((ordered, seg_plane, near))
    pieces_cot[1], pieces_cot[places - 1] = near
    landed = lax.all_to_all(ordered, DP, split_axis=0, concat_axis=0, tiled=True)
    def images_for(plane, by):
        there = ((here_x + by) % size_x * size_y + here_y) * size_core + here_core
        wanted = lax.dynamic_slice_in_dim(source_of, there * per_device, per_device)
        holder = wanted // per_device
        back_y = (here_y - holder // size_core) % size_y
        back_core = (here_core - holder) % size_core
        row = (back_y * size_core + back_core) * per_device + wanted % per_device
        row = jnp.where(holder // (size_y * size_core) == here_x, row, -1)
        plane_ids = jnp.arange(plane.shape[0], dtype=jnp.int32)
        return jnp.sum(
            jnp.where(row[:, None, None] == plane_ids[None, :, None], plane[None], 0), axis=1
        )

    images = [images_for(seg_plane, by) for by in range(size_x)]
    out_grad, grad_columns = grad_products(here, pieces_cot, out_weight)
    images, near = lax.optimization_barrier((images, near))
    images = [images[0]] + [
        lax.ppermute(images[by], "x", turn(size_x, by)) for by in range(1, size_x)
    ]
    landed, out_grad, grad_columns = lax.optimization_barrier((landed, out_grad, grad_columns))
    segments = sum(images).reshape(row_count)
    landed = landed.reshape(cuts, 2, parts_qkv, per_device * rows8, half)

    attended, probs, *partials, attended_back = attention_forward(
        landed, segments, q_gain, k_gain, out_weight, here, places
    )
    partials = [partials[0]] + [
        lax.ppermute(partials[by], "mp", turn(places, by)) for by in range(1, places)
    ]

    core = lax.axis_index("core")
    given = weight_terms(1 - core, grad_columns, attended_back, peers)
    taken = lax.ppermute(given, "core", turn(2, 1))
    kept = weight_terms(core, grad_columns, attended_back, peers)
    pair = (kept.astype(jnp.float32) + taken.astype(jnp.float32)).astype(jnp.bfloat16)
    probs, pair = lax.optimization_barrier((probs, pair))
    terms = lax.all_to_all(pair, ("x", "y"), split_axis=0, concat_axis=0, tiled=True)
    planes_grad = attention_backward(landed, probs, out_grad, attended, q_gain, k_gain)
    partials, planes_grad = lax.optimization_barrier((partials, planes_grad))
    attn_out = sum(part.astype(jnp.float32) for part in partials).astype(jnp.bfloat16)
    w_grad = jnp.sum(terms.astype(jnp.float32), axis=0)
    qkv_grad = jnp.transpose(planes_grad, (1, 0, 2))
    return (attn_out, qkv_grad, w_grad)


def solution(mesh):
    grid = Mesh(mesh.devices.reshape(4, 4, 2, 4), ("x", "y", "core", "mp"))
    rows = ("x", "y", "core", "mp")
    placed = (
        P(DP, None, "mp"),
        P(DP),
        P(),
        P("mp"),
        P("mp"),
        P(None, "mp"),
        P(rows, None),
    )
    return jax.shard_map(
        body,
        mesh=grid,
        in_specs=placed,
        out_specs=(P(rows, None), P(DP, None, "mp"), P(DP, "mp")),
        check_vma=False,
    )
```

```python
import functools
import math

import jax
import jax.numpy as jnp
from jax import lax
from jax.experimental import pallas as pl
from jax.experimental.pallas import tpu as pltpu
from jax.sharding import Mesh
from jax.sharding import PartitionSpec as P

HD = 128
BLK = 128


NORM_EPS = 1e-06
MASKED_SCORE = -1e30
LOG2_E = math.log2(math.e)
DP = ("x", "y", "core")
FORWARD_ROWS = 384
FORWARD_HEADS = 3
BACKWARD_ROWS = 768
VMEM_LIMIT = 56 * 1024 * 1024
FORWARD_VMEM = 50 * 1024 * 1024
WEIGHT_VMEM = 40 * 1024 * 1024
LITTLE = pl.CostEstimate(flops=1, bytes_accessed=1, transcendentals=0)
LARGE = pl.CostEstimate(flops=10**12, bytes_accessed=10**9, transcendentals=0)


def dot_first(left, right):
    return lax.dot_general(
        left, right, (((0,), (0,)), ((), ())), preferred_element_type=jnp.float32
    )


def dot_last(left, right):
    return lax.dot_general(
        left, right, (((1,), (1,)), ((), ())), preferred_element_type=jnp.float32
    )


def layer_norm(values, norm_gain):
    centred = values - jnp.mean(values, axis=1, keepdims=True)
    inv_scale = lax.rsqrt(jnp.mean(centred * centred, axis=1, keepdims=True) + NORM_EPS)
    normed = centred * inv_scale
    return (normed, inv_scale, (normed * norm_gain).astype(jnp.bfloat16))


def norm_backward(upstream, normed, inv_scale, norm_gain):
    scaled = upstream * norm_gain
    centred = scaled - jnp.mean(scaled, axis=1, keepdims=True)
    projection_term = normed * jnp.mean(scaled * normed, axis=1, keepdims=True)
    return (inv_scale * (centred - projection_term)).astype(jnp.bfloat16)


def in_row_order(ref, columns):
    cuts, span, _ = ref.shape[0], ref.shape[3], ref.shape[4]
    rows8 = BLK // cuts
    tiles = ref[:, 0, 0, :, columns].astype(jnp.float32).reshape(cuts, span // rows8, rows8, HD)
    return jnp.concatenate(
        [tiles[:, pos].reshape(BLK, HD) for pos in range(span // rows8)], axis=0
    )


def forward_kernel(
    groups, here_ref, q_ref, k_ref, v_ref, seg_col, seg_row, qg_ref, kg_ref, weight_ref,
    att_ref, prob_ref, *refs,
):
    at_step = pl.program_id(0)
    rows, width = att_ref.shape[0], q_ref.shape[-1]

    def attend(group):
        factor = LOG2_E / math.sqrt(HD)
        keys_image = seg_row[...]
        keys_image = jnp.where(keys_image >= 0, keys_image, -2)
        heads = [slice(first, first + HD) for first in range(0, width, HD)]
        q_hats = [layer_norm(in_row_order(q_ref, at), qg_ref[:, at])[2] for at in heads]
        k_hats = [layer_norm(in_row_order(k_ref, at), kg_ref[:, at])[2] for at in heads]
        values = [in_row_order(v_ref, at).astype(jnp.bfloat16) for at in heads]
        tasks = [
            (head, slice(start, start + FORWARD_ROWS))
            for head in range(len(heads))
            for start in range(0, rows, FORWARD_ROWS)
        ]

        def scores_of(head, block):
            return dot_last(q_hats[head][block], k_hats[head])

        ready = scores_of(*tasks[0])
        for at, (head, block) in enumerate(tasks):
            scores = ready
            if at + 1 < len(tasks):
                ready = scores_of(*tasks[at + 1])
            image = seg_col[block]
            masked = jnp.where(image == keys_image, scores, MASKED_SCORE)
            top = jnp.max(masked, axis=1, keepdims=True)
            weights = jnp.exp2((masked - top) * factor)
            totals = jnp.maximum(jnp.sum(weights, axis=1, keepdims=True), 1.0)
            scale = jnp.where(image >= 0, 1.0 / totals, 0.0)
            probs = (weights * scale).astype(jnp.bfloat16)
            prob_ref[head, block] = probs
            first = group * width + head * HD
            att_ref[block, first : first + HD] = jnp.dot(
                probs, values[head], preferred_element_type=jnp.float32
            ).astype(jnp.bfloat16)

    for group in range(groups):
        pl.when(at_step == group)(functools.partial(attend, group))

    part_refs, back_ref, turned = refs[:-2], refs[-2], refs[-1]
    places = len(part_refs)
    share = rows // places

    @pl.when(at_step == groups)
    def _():
        for by in range(places):
            first = pl.multiple_of((here_ref[0] + by) % places * share, share)
            block = att_ref[pl.ds(first, share)]
            turned[by * share : (by + 1) * share] = block
            back = (places - by) % places
            back_ref[back * share : (back + 1) * share] = block

    @pl.when(at_step >= groups)
    def _():
        sums = dot_last(turned[...], weight_ref[...]).astype(jnp.bfloat16)
        for by, part_ref in enumerate(part_refs):
            part_ref[...] = sums[by * share : (by + 1) * share]


def backward_kernel(step, q_ref, k_ref, v_ref, prob_ref, grad_ref, att_ref, qg_ref, kg_ref, out_ref):
    factor = 1.0 / math.sqrt(HD)
    q_normed, q_inv, q_hat = layer_norm(in_row_order(q_ref, slice(0, HD)), qg_ref[...])
    k_normed, k_inv, k_hat = layer_norm(in_row_order(k_ref, slice(0, HD)), kg_ref[...])
    values = in_row_order(v_ref, slice(0, HD)).astype(jnp.bfloat16)
    rows = att_ref.shape[0]
    key_sum = jnp.zeros((HD, rows), jnp.float32)
    value_sum = jnp.zeros((HD, rows), jnp.float32)
    for start in range(0, rows, step):
        block = slice(start, start + step)
        grads = grad_ref[block]
        wide = grads.astype(jnp.float32)
        probs = prob_ref[0, block]
        delta = jnp.sum(wide * att_ref[block].astype(jnp.float32), axis=1, keepdims=True)
        prob_grad = dot_last(grads, values)
        score_grad = (probs.astype(jnp.float32) * (prob_grad - delta)).astype(jnp.bfloat16)
        qn_grad = jnp.dot(score_grad, k_hat, preferred_element_type=jnp.float32) * factor
        out_ref[0, block] = norm_backward(qn_grad, q_normed[block], q_inv[block], qg_ref[...])
        value_sum += jnp.dot(
            wide.T.astype(jnp.bfloat16), probs, preferred_element_type=jnp.float32
        )
        key_sum += jnp.dot(
            q_hat[block].astype(jnp.float32).T.astype(jnp.bfloat16),
            score_grad,
            preferred_element_type=jnp.float32,
        )
    out_ref[2] = value_sum.T.astype(jnp.bfloat16)
    out_ref[1] = norm_backward(key_sum.T * factor, k_normed, k_inv, kg_ref[...])


def part_specs(cuts, span, groups, width):
    per_half = groups // 2

    def spec(part):
        def place(step, *_):
            group = jnp.minimum(step, groups - 1)
            return (0, group // per_half, part, 0, group % per_half)

        return pl.BlockSpec((cuts, 1, 1, span, width), place)

    return [spec(part) for part in range(3)]


def attention_forward(landed, segments, q_gain, k_gain, out_weight, here, places):
    cuts, _, _, span, half = landed.shape
    rows, heads = cuts * span, 2 * half // HD
    groups, width = heads // FORWARD_HEADS, FORWARD_HEADS * HD
    d_out = out_weight.shape[0]
    blocks = 4
    share = rows // places
    gain_spec = pl.BlockSpec((1, width), lambda step, here: (0, jnp.minimum(step, groups - 1)))

    def column(step):
        return jnp.maximum(step - groups, 0)

    return pl.pallas_call(
        functools.partial(forward_kernel, groups),
        grid_spec=pltpu.PrefetchScalarGridSpec(
        num_scalar_prefetch=1,
        grid=(groups + blocks,),
        in_specs=part_specs(cuts, span, groups, width)
        + [
            pl.BlockSpec((rows, 1), lambda step, here: (0, 0)),
            pl.BlockSpec((1, rows), lambda step, here: (0, 0)),
            gain_spec,
            gain_spec,
            pl.BlockSpec((d_out // blocks, heads * HD), lambda step, here: (column(step), 0)),
        ],
        out_specs=[
            pl.BlockSpec((rows, heads * HD), lambda step, here: (0, 0)),
            pl.BlockSpec(
                (FORWARD_HEADS, rows, rows), lambda step, here: (jnp.minimum(step, groups - 1), 0, 0)
            ),
        ]
        + [pl.BlockSpec((share, d_out // blocks), lambda step, here: (0, column(step)))] * places
        + [pl.BlockSpec((rows, heads * HD), lambda step, here: (0, 0))],
        scratch_shapes=[pltpu.VMEM((rows, heads * HD), jnp.bfloat16)],
        ),
        out_shape=[
            jax.ShapeDtypeStruct((rows, heads * HD), jnp.bfloat16),
            jax.ShapeDtypeStruct((heads, rows, rows), jnp.bfloat16),
        ]
        + [jax.ShapeDtypeStruct((share, d_out), jnp.bfloat16)] * places
        + [jax.ShapeDtypeStruct((rows, heads * HD), jnp.bfloat16)],
        compiler_params=pltpu.CompilerParams(vmem_limit_bytes=FORWARD_VMEM),
        cost_estimate=pl.CostEstimate(
            flops=4 * heads * rows * rows * HD + 2 * rows * d_out * heads * HD,
            bytes_accessed=2 * heads * rows * (rows + 4 * HD) + 4 * rows * d_out,
            transcendentals=heads * rows * rows,
        ),
        name="attention_forward",
    )(
        here.reshape(1).astype(jnp.int32),
        landed,
        landed,
        landed,
        segments[:, None],
        segments[None, :],
        q_gain[None, :],
        k_gain[None, :],
        out_weight,
    )


def attention_backward(landed, probs, out_grad, attended, q_gain, k_gain):
    cuts, _, _, span, half = landed.shape
    rows, heads = cuts * span, 2 * half // HD
    gain_spec = pl.BlockSpec((1, HD), lambda head: (0, head))
    row_spec = pl.BlockSpec((rows, HD), lambda head: (0, head))
    return pl.pallas_call(
        functools.partial(backward_kernel, BACKWARD_ROWS),
        grid=(heads,),
        in_specs=part_specs(cuts, span, heads, HD)
        + [
            pl.BlockSpec((1, rows, rows), lambda head: (head, 0, 0)),
            row_spec,
            row_spec,
            gain_spec,
            gain_spec,
        ],
        out_specs=pl.BlockSpec((3, rows, HD), lambda head: (0, 0, head)),
        out_shape=jax.ShapeDtypeStruct((3, rows, heads * HD), jnp.bfloat16),
        compiler_params=pltpu.CompilerParams(vmem_limit_bytes=VMEM_LIMIT),
        cost_estimate=LARGE,
        name="attention_backward",
    )(landed, landed, landed, probs, out_grad, attended, q_gain[None, :], k_gain[None, :])


def cut_kernel(rows_ref, out_ref):
    cuts, sides, _, span, half = out_ref.shape
    rows8 = BLK // cuts
    tiles = rows_ref[0].astype(jnp.float32).reshape(span // rows8, cuts, rows8, sides * half)
    for cut in range(cuts):
        rows = tiles[:, cut].reshape(span, sides * half).astype(jnp.bfloat16)
        for side in range(sides):
            out_ref[cut, side, 0] = rows[:, side * half : (side + 1) * half]


def cut_blocks(planes, cuts):
    parts, rows, width = planes.shape
    span, half = rows // cuts, width // 2
    return pl.pallas_call(
        cut_kernel,
        grid=(parts,),
        in_specs=[pl.BlockSpec((1, rows, width), lambda part: (part, 0, 0))],
        out_specs=pl.BlockSpec((cuts, 2, 1, span, half), lambda part: (0, 0, part, 0, 0)),
        out_shape=jax.ShapeDtypeStruct((cuts, 2, parts, span, half), jnp.bfloat16),
        compiler_params=pltpu.CompilerParams(vmem_limit_bytes=VMEM_LIMIT),
        cost_estimate=pl.CostEstimate(
            flops=0, bytes_accessed=4 * parts * rows * width, transcendentals=0
        ),
        name="cut_blocks",
    )(planes)


def grad_kernel(here_ref, *refs):
    pieces, (weight_ref, grad_ref, columns_ref, total) = refs[:-4], refs[-4:]
    places, step = len(pieces), pl.program_id(0)
    rows = jnp.concatenate([piece[...].astype(jnp.float32) for piece in pieces], axis=0)
    columns_ref[...] = rows.T.astype(jnp.bfloat16)
    product = jnp.dot(
        rows.astype(jnp.bfloat16), weight_ref[...], preferred_element_type=jnp.float32
    )

    @pl.when(step == 0)
    def _():
        total[...] = product

    @pl.when(step > 0)
    def _():
        total[...] += product

    @pl.when(step == pl.num_programs(0) - 1)
    def _():
        share = pieces[0].shape[0]
        for back in range(places):
            first = pl.multiple_of((here_ref[0] + places - back) % places * share, share)
            grad_ref[pl.ds(first, share)] = total[back * share : (back + 1) * share].astype(
                jnp.bfloat16
            )


def grad_products(here, pieces, out_weight):
    places = len(pieces)
    share, d_out = pieces[0].shape
    width = out_weight.shape[1]
    rows, step = places * share, 768
    return pl.pallas_call(
        grad_kernel,
        grid_spec=pltpu.PrefetchScalarGridSpec(
            num_scalar_prefetch=1,
            grid=(d_out // step,),
            in_specs=[pl.BlockSpec((share, step), lambda at, here: (0, at))] * places
            + [pl.BlockSpec((step, width), lambda at, here: (at, 0))],
            out_specs=[
                pl.BlockSpec((rows, width), lambda at, here: (0, 0)),
                pl.BlockSpec((step, rows), lambda at, here: (at, 0)),
            ],
            scratch_shapes=[pltpu.VMEM((rows, width), jnp.float32)],
        ),
        out_shape=[
            jax.ShapeDtypeStruct((rows, width), jnp.bfloat16),
            jax.ShapeDtypeStruct((d_out, rows), jnp.bfloat16),
        ],
        compiler_params=pltpu.CompilerParams(vmem_limit_bytes=VMEM_LIMIT),
        cost_estimate=LITTLE,
        name="grad_products",
    )(here.reshape(1).astype(jnp.int32), *pieces, out_weight)


def weight_kernel(core_ref, cot_ref, att_ref, out_ref):
    peers, _, share, rows = cot_ref.shape
    terms = jnp.dot(
        cot_ref[...].reshape(peers * share, rows),
        att_ref[...],
        preferred_element_type=jnp.float32,
    )
    out_ref[...] = terms.astype(jnp.bfloat16).reshape(out_ref.shape)


def weight_terms(parity, grad_columns, attended, peers):
    d_out, rows = grad_columns.shape
    width = attended.shape[1]
    share = d_out // peers
    step = peers // 4
    block = pl.BlockSpec((step, share, width), lambda at, core: (at, 0, 0))
    return pl.pallas_call(
        weight_kernel,
        grid_spec=pltpu.PrefetchScalarGridSpec(
            num_scalar_prefetch=1,
            grid=(2,),
            in_specs=[
                pl.BlockSpec((step, 1, share, rows), lambda at, core: (at, core[0], 0, 0)),
                pl.BlockSpec((rows, width), lambda at, core: (0, 0)),
            ],
            out_specs=block,
        ),
        out_shape=jax.ShapeDtypeStruct((peers // 2, share, width), jnp.bfloat16),
        compiler_params=pltpu.CompilerParams(vmem_limit_bytes=WEIGHT_VMEM),
        cost_estimate=LARGE,
        name="weight_terms",
    )(
        parity.reshape(1).astype(jnp.int32),
        grad_columns.reshape(peers // 2, 2, share, rows),
        attended,
    )


def turn(size, by):
    return [(at, (at + by) % size) for at in range(size)]


def gathered(own, axis):
    size = lax.axis_size(axis)
    return jnp.stack([own] + [lax.ppermute(own, axis, turn(size, by)) for by in range(1, size)])


def body(qkv, segment_ids, block_dest, q_gain, k_gain, out_weight, cotangent):
    peers = lax.axis_size(DP)
    my_index = lax.axis_index(DP)
    row_count, parts_qkv, col_width = qkv.shape
    per_device = row_count // BLK
    n_blocks = block_dest.shape[0]
    cuts = peers // 2
    rows8 = BLK // cuts
    half = col_width // 2

    all_ids = jnp.arange(n_blocks, dtype=jnp.int32)
    source_of = jnp.sum(
        (block_dest[None, :] == all_ids[:, None]).astype(jnp.int32) * all_ids[None, :], axis=1
    )
    size_x, size_y, size_core = (lax.axis_size(axis) for axis in DP)
    here_x, here_y, here_core = (lax.axis_index(axis) for axis in DP)
    seg_plane = gathered(gathered(segment_ids.reshape(per_device, BLK), "core"), "y")
    seg_plane = seg_plane.reshape(size_y * size_core * per_device, BLK)

    sources = source_of.reshape(peers, 1, per_device)
    part_ids = jnp.arange(parts_qkv, dtype=jnp.int32)[None, :, None]
    piece_of = (
        (sources // per_device) * (parts_qkv * per_device)
        + part_ids * per_device
        + sources % per_device
    ).reshape(-1)

    places = lax.axis_size("mp")
    here = lax.axis_index("mp")
    pieces_cot = [cotangent] + [
        lax.ppermute(cotangent, "mp", turn(places, by)) for by in range(1, places)
    ]

    planes = jnp.transpose(qkv, (1, 0, 2))
    pieces = cut_blocks(planes, cuts).reshape(peers, parts_qkv, per_device * rows8, half)
    spread = lax.all_to_all(pieces, DP, split_axis=0, concat_axis=0, tiled=True)
    ordered = jnp.take(
        spread.reshape(n_blocks * parts_qkv, rows8, half), piece_of, axis=0, mode="clip"
    ).reshape(pieces.shape)
    near = (pieces_cot[1], pieces_cot[places - 1])
    ordered, seg_plane, near = lax.optimization_barrier((ordered, seg_plane, near))
    pieces_cot[1], pieces_cot[places - 1] = near
    landed = lax.all_to_all(ordered, DP, split_axis=0, concat_axis=0, tiled=True)
    def images_for(plane, by):
        there = ((here_x + by) % size_x * size_y + here_y) * size_core + here_core
        wanted = lax.dynamic_slice_in_dim(source_of, there * per_device, per_device)
        holder = wanted // per_device
        back_y = (here_y - holder // size_core) % size_y
        back_core = (here_core - holder) % size_core
        row = (back_y * size_core + back_core) * per_device + wanted % per_device
        row = jnp.where(holder // (size_y * size_core) == here_x, row, -1)
        plane_ids = jnp.arange(plane.shape[0], dtype=jnp.int32)
        return jnp.sum(
            jnp.where(row[:, None, None] == plane_ids[None, :, None], plane[None], 0), axis=1
        )

    images = [images_for(seg_plane, by) for by in range(size_x)]
    out_grad, grad_columns = grad_products(here, pieces_cot, out_weight)
    images, near = lax.optimization_barrier((images, near))
    images = [images[0]] + [
        lax.ppermute(images[by], "x", turn(size_x, by)) for by in range(1, size_x)
    ]
    landed, out_grad, grad_columns = lax.optimization_barrier((landed, out_grad, grad_columns))
    segments = sum(images).reshape(row_count)
    landed = landed.reshape(cuts, 2, parts_qkv, per_device * rows8, half)

    attended, probs, *partials, attended_back = attention_forward(
        landed, segments, q_gain, k_gain, out_weight, here, places
    )
    opposite = places // 2
    for by in range(1, places):
        if by != opposite:
            partials[by] = lax.ppermute(partials[by], "mp", turn(places, by))

    core = lax.axis_index("core")
    given = weight_terms(1 - core, grad_columns, attended_back, peers)
    taken = lax.ppermute(given, "core", turn(2, 1))
    kept = weight_terms(core, grad_columns, attended_back, peers)
    pair = (kept.astype(jnp.float32) + taken.astype(jnp.float32)).astype(jnp.bfloat16)
    pair, partials[opposite] = lax.optimization_barrier((pair, partials[opposite]))
    partials[opposite] = lax.ppermute(partials[opposite], "mp", turn(places, opposite))
    probs, pair = lax.optimization_barrier((probs, pair))
    terms = lax.all_to_all(pair, ("x", "y"), split_axis=0, concat_axis=0, tiled=True)
    planes_grad = attention_backward(landed, probs, out_grad, attended, q_gain, k_gain)
    partials, planes_grad = lax.optimization_barrier((partials, planes_grad))
    attn_out = sum(part.astype(jnp.float32) for part in partials).astype(jnp.bfloat16)
    w_grad = jnp.sum(terms.astype(jnp.float32), axis=0)
    qkv_grad = jnp.transpose(planes_grad, (1, 0, 2))
    return (attn_out, qkv_grad, w_grad)


def solution(mesh):
    grid = Mesh(mesh.devices.reshape(4, 4, 2, 4), ("x", "y", "core", "mp"))
    rows = ("x", "y", "core", "mp")
    placed = (
        P(DP, None, "mp"),
        P(DP),
        P(),
        P("mp"),
        P("mp"),
        P(None, "mp"),
        P(rows, None),
    )
    return jax.shard_map(
        body,
        mesh=grid,
        in_specs=placed,
        out_specs=(P(rows, None), P(DP, None, "mp"), P(DP, "mp")),
        check_vma=False,
    )
```

```python
import functools
import math

import jax
import jax.numpy as jnp
from jax import lax
from jax.experimental import pallas as pl
from jax.experimental.pallas import tpu as pltpu
from jax.sharding import Mesh
from jax.sharding import PartitionSpec as P

HD = 128
BLK = 128


NORM_EPS = 1e-06
MASKED_SCORE = -1e30
LOG2_E = math.log2(math.e)
DP = ("x", "y", "core")
FORWARD_ROWS = 384
FORWARD_HEADS = 3
BACKWARD_ROWS = 768
VMEM_LIMIT = 56 * 1024 * 1024
FORWARD_VMEM = 50 * 1024 * 1024
WEIGHT_VMEM = 40 * 1024 * 1024
LITTLE = pl.CostEstimate(flops=1, bytes_accessed=1, transcendentals=0)
LARGE = pl.CostEstimate(flops=10**12, bytes_accessed=10**9, transcendentals=0)


def dot_first(left, right):
    return lax.dot_general(
        left, right, (((0,), (0,)), ((), ())), preferred_element_type=jnp.float32
    )


def dot_last(left, right):
    return lax.dot_general(
        left, right, (((1,), (1,)), ((), ())), preferred_element_type=jnp.float32
    )


def layer_norm(values, norm_gain):
    centred = values - jnp.mean(values, axis=1, keepdims=True)
    inv_scale = lax.rsqrt(jnp.mean(centred * centred, axis=1, keepdims=True) + NORM_EPS)
    normed = centred * inv_scale
    return (normed, inv_scale, (normed * norm_gain).astype(jnp.bfloat16))


def norm_backward(upstream, normed, inv_scale, norm_gain):
    scaled = upstream * norm_gain
    centred = scaled - jnp.mean(scaled, axis=1, keepdims=True)
    projection_term = normed * jnp.mean(scaled * normed, axis=1, keepdims=True)
    return (inv_scale * (centred - projection_term)).astype(jnp.bfloat16)


def in_row_order(ref, columns):
    cuts, span, _ = ref.shape[0], ref.shape[3], ref.shape[4]
    rows8 = BLK // cuts
    tiles = ref[:, 0, 0, :, columns].astype(jnp.float32).reshape(cuts, span // rows8, rows8, HD)
    return jnp.concatenate(
        [tiles[:, pos].reshape(BLK, HD) for pos in range(span // rows8)], axis=0
    )


def forward_kernel(
    groups, here_ref, q_ref, k_ref, v_ref, seg_col, seg_row, qg_ref, kg_ref, weight_ref,
    att_ref, prob_ref, *refs,
):
    at_step = pl.program_id(0)
    rows, width = att_ref.shape[0], q_ref.shape[-1]

    def attend(group):
        factor = LOG2_E / math.sqrt(HD)
        keys_image = seg_row[...]
        keys_image = jnp.where(keys_image >= 0, keys_image, -2)
        heads = [slice(first, first + HD) for first in range(0, width, HD)]
        q_hats = [layer_norm(in_row_order(q_ref, at), qg_ref[:, at])[2] for at in heads]
        k_hats = [layer_norm(in_row_order(k_ref, at), kg_ref[:, at])[2] for at in heads]
        values = [in_row_order(v_ref, at).astype(jnp.bfloat16) for at in heads]
        tasks = [
            (head, slice(start, start + FORWARD_ROWS))
            for head in range(len(heads))
            for start in range(0, rows, FORWARD_ROWS)
        ]

        def scores_of(head, block):
            return dot_last(q_hats[head][block], k_hats[head])

        ready = scores_of(*tasks[0])
        for at, (head, block) in enumerate(tasks):
            scores = ready
            if at + 1 < len(tasks):
                ready = scores_of(*tasks[at + 1])
            image = seg_col[block]
            masked = jnp.where(image == keys_image, scores, MASKED_SCORE)
            top = jnp.max(masked, axis=1, keepdims=True)
            weights = jnp.exp2((masked - top) * factor)
            totals = jnp.maximum(jnp.sum(weights, axis=1, keepdims=True), 1.0)
            scale = jnp.where(image >= 0, 1.0 / totals, 0.0)
            probs = (weights * scale).astype(jnp.bfloat16)
            prob_ref[head, block] = probs
            first = group * width + head * HD
            att_ref[block, first : first + HD] = jnp.dot(
                probs, values[head], preferred_element_type=jnp.float32
            ).astype(jnp.bfloat16)

    for group in range(groups):
        pl.when(at_step == group)(functools.partial(attend, group))

    part_refs, back_ref, turned = refs[:-2], refs[-2], refs[-1]
    places = len(part_refs)
    share = rows // places

    @pl.when(at_step == groups)
    def _():
        for by in range(places):
            first = pl.multiple_of((here_ref[0] + by) % places * share, share)
            block = att_ref[pl.ds(first, share)]
            turned[by * share : (by + 1) * share] = block
            back = (places - by) % places
            back_ref[back * share : (back + 1) * share] = block

    @pl.when(at_step >= groups)
    def _():
        sums = dot_last(turned[...], weight_ref[...]).astype(jnp.bfloat16)
        for by, part_ref in enumerate(part_refs):
            part_ref[...] = sums[by * share : (by + 1) * share]


def backward_kernel(step, q_ref, k_ref, v_ref, prob_ref, grad_ref, att_ref, qg_ref, kg_ref, out_ref):
    factor = 1.0 / math.sqrt(HD)
    q_normed, q_inv, q_hat = layer_norm(in_row_order(q_ref, slice(0, HD)), qg_ref[...])
    k_normed, k_inv, k_hat = layer_norm(in_row_order(k_ref, slice(0, HD)), kg_ref[...])
    values = in_row_order(v_ref, slice(0, HD)).astype(jnp.bfloat16)
    rows = att_ref.shape[0]
    key_sum = jnp.zeros((HD, rows), jnp.float32)
    value_sum = jnp.zeros((HD, rows), jnp.float32)
    for start in range(0, rows, step):
        block = slice(start, start + step)
        grads = grad_ref[block]
        wide = grads.astype(jnp.float32)
        probs = prob_ref[0, block]
        delta = jnp.sum(wide * att_ref[block].astype(jnp.float32), axis=1, keepdims=True)
        prob_grad = dot_last(grads, values)
        score_grad = (probs.astype(jnp.float32) * (prob_grad - delta)).astype(jnp.bfloat16)
        qn_grad = jnp.dot(score_grad, k_hat, preferred_element_type=jnp.float32) * factor
        out_ref[0, block] = norm_backward(qn_grad, q_normed[block], q_inv[block], qg_ref[...])
        value_sum += jnp.dot(
            wide.T.astype(jnp.bfloat16), probs, preferred_element_type=jnp.float32
        )
        key_sum += jnp.dot(
            q_hat[block].astype(jnp.float32).T.astype(jnp.bfloat16),
            score_grad,
            preferred_element_type=jnp.float32,
        )
    out_ref[2] = value_sum.T.astype(jnp.bfloat16)
    out_ref[1] = norm_backward(key_sum.T * factor, k_normed, k_inv, kg_ref[...])


def part_specs(cuts, span, groups, width):
    per_half = groups // 2

    def spec(part):
        def place(step, *_):
            group = jnp.minimum(step, groups - 1)
            return (0, group // per_half, part, 0, group % per_half)

        return pl.BlockSpec((cuts, 1, 1, span, width), place)

    return [spec(part) for part in range(3)]


def attention_forward(landed, segments, q_gain, k_gain, out_weight, here, places):
    cuts, _, _, span, half = landed.shape
    rows, heads = cuts * span, 2 * half // HD
    groups, width = heads // FORWARD_HEADS, FORWARD_HEADS * HD
    d_out = out_weight.shape[0]
    blocks = 3
    share = rows // places
    gain_spec = pl.BlockSpec((1, width), lambda step, here: (0, jnp.minimum(step, groups - 1)))

    def column(step):
        return jnp.maximum(step - groups, 0)

    return pl.pallas_call(
        functools.partial(forward_kernel, groups),
        grid_spec=pltpu.PrefetchScalarGridSpec(
        num_scalar_prefetch=1,
        grid=(groups + blocks,),
        in_specs=part_specs(cuts, span, groups, width)
        + [
            pl.BlockSpec((rows, 1), lambda step, here: (0, 0)),
            pl.BlockSpec((1, rows), lambda step, here: (0, 0)),
            gain_spec,
            gain_spec,
            pl.BlockSpec((d_out // blocks, heads * HD), lambda step, here: (column(step), 0)),
        ],
        out_specs=[
            pl.BlockSpec((rows, heads * HD), lambda step, here: (0, 0)),
            pl.BlockSpec(
                (FORWARD_HEADS, rows, rows), lambda step, here: (jnp.minimum(step, groups - 1), 0, 0)
            ),
        ]
        + [pl.BlockSpec((share, d_out // blocks), lambda step, here: (0, column(step)))] * places
        + [pl.BlockSpec((rows, heads * HD), lambda step, here: (0, 0))],
        scratch_shapes=[pltpu.VMEM((rows, heads * HD), jnp.bfloat16)],
        ),
        out_shape=[
            jax.ShapeDtypeStruct((rows, heads * HD), jnp.bfloat16),
            jax.ShapeDtypeStruct((heads, rows, rows), jnp.bfloat16),
        ]
        + [jax.ShapeDtypeStruct((share, d_out), jnp.bfloat16)] * places
        + [jax.ShapeDtypeStruct((rows, heads * HD), jnp.bfloat16)],
        compiler_params=pltpu.CompilerParams(vmem_limit_bytes=FORWARD_VMEM),
        cost_estimate=pl.CostEstimate(
            flops=4 * heads * rows * rows * HD + 2 * rows * d_out * heads * HD,
            bytes_accessed=2 * heads * rows * (rows + 4 * HD) + 4 * rows * d_out,
            transcendentals=heads * rows * rows,
        ),
        name="attention_forward",
    )(
        here.reshape(1).astype(jnp.int32),
        landed,
        landed,
        landed,
        segments[:, None],
        segments[None, :],
        q_gain[None, :],
        k_gain[None, :],
        out_weight,
    )


def attention_backward(landed, probs, out_grad, attended, q_gain, k_gain):
    cuts, _, _, span, half = landed.shape
    rows, heads = cuts * span, 2 * half // HD
    gain_spec = pl.BlockSpec((1, HD), lambda head: (0, head))
    row_spec = pl.BlockSpec((rows, HD), lambda head: (0, head))
    return pl.pallas_call(
        functools.partial(backward_kernel, BACKWARD_ROWS),
        grid=(heads,),
        in_specs=part_specs(cuts, span, heads, HD)
        + [
            pl.BlockSpec((1, rows, rows), lambda head: (head, 0, 0)),
            row_spec,
            row_spec,
            gain_spec,
            gain_spec,
        ],
        out_specs=pl.BlockSpec((3, rows, HD), lambda head: (0, 0, head)),
        out_shape=jax.ShapeDtypeStruct((3, rows, heads * HD), jnp.bfloat16),
        compiler_params=pltpu.CompilerParams(vmem_limit_bytes=VMEM_LIMIT),
        cost_estimate=LARGE,
        name="attention_backward",
    )(landed, landed, landed, probs, out_grad, attended, q_gain[None, :], k_gain[None, :])


def cut_kernel(rows_ref, out_ref):
    cuts, sides, _, span, half = out_ref.shape
    rows8 = BLK // cuts
    tiles = rows_ref[0].astype(jnp.float32).reshape(span // rows8, cuts, rows8, sides * half)
    for cut in range(cuts):
        rows = tiles[:, cut].reshape(span, sides * half).astype(jnp.bfloat16)
        for side in range(sides):
            out_ref[cut, side, 0] = rows[:, side * half : (side + 1) * half]


def cut_blocks(planes, cuts):
    parts, rows, width = planes.shape
    span, half = rows // cuts, width // 2
    return pl.pallas_call(
        cut_kernel,
        grid=(parts,),
        in_specs=[pl.BlockSpec((1, rows, width), lambda part: (part, 0, 0))],
        out_specs=pl.BlockSpec((cuts, 2, 1, span, half), lambda part: (0, 0, part, 0, 0)),
        out_shape=jax.ShapeDtypeStruct((cuts, 2, parts, span, half), jnp.bfloat16),
        compiler_params=pltpu.CompilerParams(vmem_limit_bytes=VMEM_LIMIT),
        cost_estimate=pl.CostEstimate(
            flops=0, bytes_accessed=4 * parts * rows * width, transcendentals=0
        ),
        name="cut_blocks",
    )(planes)


def grad_kernel(here_ref, *refs):
    pieces, (weight_ref, grad_ref, columns_ref, total) = refs[:-4], refs[-4:]
    places, step = len(pieces), pl.program_id(0)
    rows = jnp.concatenate([piece[...].astype(jnp.float32) for piece in pieces], axis=0)
    columns_ref[...] = rows.T.astype(jnp.bfloat16)
    product = jnp.dot(
        rows.astype(jnp.bfloat16), weight_ref[...], preferred_element_type=jnp.float32
    )

    @pl.when(step == 0)
    def _():
        total[...] = product

    @pl.when(step > 0)
    def _():
        total[...] += product

    @pl.when(step == pl.num_programs(0) - 1)
    def _():
        share = pieces[0].shape[0]
        for back in range(places):
            first = pl.multiple_of((here_ref[0] + places - back) % places * share, share)
            grad_ref[pl.ds(first, share)] = total[back * share : (back + 1) * share].astype(
                jnp.bfloat16
            )


def grad_products(here, pieces, out_weight):
    places = len(pieces)
    share, d_out = pieces[0].shape
    width = out_weight.shape[1]
    rows, step = places * share, 768
    return pl.pallas_call(
        grad_kernel,
        grid_spec=pltpu.PrefetchScalarGridSpec(
            num_scalar_prefetch=1,
            grid=(d_out // step,),
            in_specs=[pl.BlockSpec((share, step), lambda at, here: (0, at))] * places
            + [pl.BlockSpec((step, width), lambda at, here: (at, 0))],
            out_specs=[
                pl.BlockSpec((rows, width), lambda at, here: (0, 0)),
                pl.BlockSpec((step, rows), lambda at, here: (at, 0)),
            ],
            scratch_shapes=[pltpu.VMEM((rows, width), jnp.float32)],
        ),
        out_shape=[
            jax.ShapeDtypeStruct((rows, width), jnp.bfloat16),
            jax.ShapeDtypeStruct((d_out, rows), jnp.bfloat16),
        ],
        compiler_params=pltpu.CompilerParams(vmem_limit_bytes=VMEM_LIMIT),
        cost_estimate=LITTLE,
        name="grad_products",
    )(here.reshape(1).astype(jnp.int32), *pieces, out_weight)


def weight_kernel(core_ref, cot_ref, att_ref, out_ref):
    peers, _, share, rows = cot_ref.shape
    terms = jnp.dot(
        cot_ref[...].reshape(peers * share, rows),
        att_ref[...],
        preferred_element_type=jnp.float32,
    )
    out_ref[...] = terms.astype(jnp.bfloat16).reshape(out_ref.shape)


def weight_terms(parity, grad_columns, attended, peers):
    d_out, rows = grad_columns.shape
    width = attended.shape[1]
    share = d_out // peers
    step = peers // 4
    block = pl.BlockSpec((step, share, width), lambda at, core: (at, 0, 0))
    return pl.pallas_call(
        weight_kernel,
        grid_spec=pltpu.PrefetchScalarGridSpec(
            num_scalar_prefetch=1,
            grid=(2,),
            in_specs=[
                pl.BlockSpec((step, 1, share, rows), lambda at, core: (at, core[0], 0, 0)),
                pl.BlockSpec((rows, width), lambda at, core: (0, 0)),
            ],
            out_specs=block,
        ),
        out_shape=jax.ShapeDtypeStruct((peers // 2, share, width), jnp.bfloat16),
        compiler_params=pltpu.CompilerParams(vmem_limit_bytes=WEIGHT_VMEM),
        cost_estimate=LARGE,
        name="weight_terms",
    )(
        parity.reshape(1).astype(jnp.int32),
        grad_columns.reshape(peers // 2, 2, share, rows),
        attended,
    )


def turn(size, by):
    return [(at, (at + by) % size) for at in range(size)]


def gathered(own, axis):
    size = lax.axis_size(axis)
    return jnp.stack([own] + [lax.ppermute(own, axis, turn(size, by)) for by in range(1, size)])


def body(qkv, segment_ids, block_dest, q_gain, k_gain, out_weight, cotangent):
    peers = lax.axis_size(DP)
    my_index = lax.axis_index(DP)
    row_count, parts_qkv, col_width = qkv.shape
    per_device = row_count // BLK
    n_blocks = block_dest.shape[0]
    cuts = peers // 2
    rows8 = BLK // cuts
    half = col_width // 2

    all_ids = jnp.arange(n_blocks, dtype=jnp.int32)
    source_of = jnp.sum(
        (block_dest[None, :] == all_ids[:, None]).astype(jnp.int32) * all_ids[None, :], axis=1
    )
    size_x, size_y, size_core = (lax.axis_size(axis) for axis in DP)
    here_x, here_y, here_core = (lax.axis_index(axis) for axis in DP)
    seg_plane = gathered(gathered(segment_ids.reshape(per_device, BLK), "core"), "y")
    seg_plane = seg_plane.reshape(size_y * size_core * per_device, BLK)

    sources = source_of.reshape(peers, 1, per_device)
    part_ids = jnp.arange(parts_qkv, dtype=jnp.int32)[None, :, None]
    piece_of = (
        (sources // per_device) * (parts_qkv * per_device)
        + part_ids * per_device
        + sources % per_device
    ).reshape(-1)

    places = lax.axis_size("mp")
    here = lax.axis_index("mp")
    pieces_cot = [cotangent] + [
        lax.ppermute(cotangent, "mp", turn(places, by)) for by in range(1, places)
    ]

    planes = jnp.transpose(qkv, (1, 0, 2))
    pieces = cut_blocks(planes, cuts).reshape(peers, parts_qkv, per_device * rows8, half)
    spread = lax.all_to_all(pieces, DP, split_axis=0, concat_axis=0, tiled=True)
    ordered = jnp.take(
        spread.reshape(n_blocks * parts_qkv, rows8, half), piece_of, axis=0, mode="clip"
    ).reshape(pieces.shape)
    near = (pieces_cot[1], pieces_cot[places - 1])
    ordered, seg_plane, near = lax.optimization_barrier((ordered, seg_plane, near))
    pieces_cot[1], pieces_cot[places - 1] = near
    landed = lax.all_to_all(ordered, DP, split_axis=0, concat_axis=0, tiled=True)
    def images_for(plane, by):
        there = ((here_x + by) % size_x * size_y + here_y) * size_core + here_core
        wanted = lax.dynamic_slice_in_dim(source_of, there * per_device, per_device)
        holder = wanted // per_device
        back_y = (here_y - holder // size_core) % size_y
        back_core = (here_core - holder) % size_core
        row = (back_y * size_core + back_core) * per_device + wanted % per_device
        row = jnp.where(holder // (size_y * size_core) == here_x, row, -1)
        plane_ids = jnp.arange(plane.shape[0], dtype=jnp.int32)
        return jnp.sum(
            jnp.where(row[:, None, None] == plane_ids[None, :, None], plane[None], 0), axis=1
        )

    images = [images_for(seg_plane, by) for by in range(size_x)]
    out_grad, grad_columns = grad_products(here, pieces_cot, out_weight)
    images, near = lax.optimization_barrier((images, near))
    images = [images[0]] + [
        lax.ppermute(images[by], "x", turn(size_x, by)) for by in range(1, size_x)
    ]
    landed, out_grad, grad_columns = lax.optimization_barrier((landed, out_grad, grad_columns))
    segments = sum(images).reshape(row_count)
    landed = landed.reshape(cuts, 2, parts_qkv, per_device * rows8, half)

    attended, probs, *partials, attended_back = attention_forward(
        landed, segments, q_gain, k_gain, out_weight, here, places
    )
    opposite = places // 2
    for by in range(1, places):
        if by != opposite:
            partials[by] = lax.ppermute(partials[by], "mp", turn(places, by))

    core = lax.axis_index("core")
    given = weight_terms(1 - core, grad_columns, attended_back, peers)
    taken = lax.ppermute(given, "core", turn(2, 1))
    kept = weight_terms(core, grad_columns, attended_back, peers)
    pair = (kept.astype(jnp.float32) + taken.astype(jnp.float32)).astype(jnp.bfloat16)
    pair, partials[opposite] = lax.optimization_barrier((pair, partials[opposite]))
    partials[opposite] = lax.ppermute(partials[opposite], "mp", turn(places, opposite))
    probs, pair = lax.optimization_barrier((probs, pair))
    terms = lax.all_to_all(pair, ("x", "y"), split_axis=0, concat_axis=0, tiled=True)
    planes_grad = attention_backward(landed, probs, out_grad, attended, q_gain, k_gain)
    partials, planes_grad = lax.optimization_barrier((partials, planes_grad))
    attn_out = sum(part.astype(jnp.float32) for part in partials).astype(jnp.bfloat16)
    w_grad = jnp.sum(terms.astype(jnp.float32), axis=0)
    qkv_grad = jnp.transpose(planes_grad, (1, 0, 2))
    return (attn_out, qkv_grad, w_grad)


def solution(mesh):
    grid = Mesh(mesh.devices.reshape(4, 4, 2, 4), ("x", "y", "core", "mp"))
    rows = ("x", "y", "core", "mp")
    placed = (
        P(DP, None, "mp"),
        P(DP),
        P(),
        P("mp"),
        P("mp"),
        P(None, "mp"),
        P(rows, None),
    )
    return jax.shard_map(
        body,
        mesh=grid,
        in_specs=placed,
        out_specs=(P(rows, None), P(DP, None, "mp"), P(DP, "mp")),
        check_vma=False,
    )
```
